32 devices in a mesh: groups: 2 (over x), tiles: 16 (over z, y, core).
Axes of the slice: x: 2, y: 2, z: 4, core: 2. Of those that a mesh axis runs over, the one named last changes fastest.
Arguments:
- features: bfloat16 [512, 128, 128], P(('groups', 'tiles')), parts along dimension 0, may hold values from -40 to 40
- window_offsets: int32 [4], P('groups'), parts along dimension 0, may hold values from 0 to 31
- self_project: bfloat16 [128, 384], replicated, may hold values from -0.5 to 0.5
- self_merge: bfloat16 [128, 128], replicated, may hold values from -0.5 to 0.5
- cross_project: bfloat16 [128, 384], replicated, may hold values from -0.5 to 0.5
- cross_merge: bfloat16 [128, 128], replicated, may hold values from -0.5 to 0.5
- feed_in: bfloat16 [256, 512], replicated, may hold values from -0.375 to 0.375
- feed_out: bfloat16 [512, 128], replicated, may hold values from -0.25 to 0.25
- norm_gains: float32 [3, 128], replicated, may hold values from 0.1 to 1.9
- result_grad: float32 [512, 128, 128], P(('groups', 'tiles')), parts along dimension 0, may hold values from -6 to 6
Outputs:
- result: bfloat16 [512, 128, 128], P(('groups', 'tiles')), parts along dimension 0
- features_grad: float32 [512, 128, 128], P(('groups', 'tiles')), parts along dimension 0
- self_project_grad: float32 [256, 384], P(('groups', 'tiles')), parts along dimension 0
- self_merge_grad: float32 [256, 128], P(('groups', 'tiles')), parts along dimension 0
- cross_project_grad: float32 [256, 384], P(('groups', 'tiles')), parts along dimension 0
- cross_merge_grad: float32 [256, 128], P(('groups', 'tiles')), parts along dimension 0
- feed_in_grad: float32 [512, 512], P(('groups', 'tiles')), parts along dimension 0
- feed_out_grad: float32 [1024, 128], P(('groups', 'tiles')), parts along dimension 0
- norm_gains_grad: float32 [6, 128], P('groups', 'tiles'), parts along dimension 0
The draws below stay inside these ranges and needn't reach their ends.
There are 2 independent parts, one for each index of `groups`. The reference program is written for one: setup_inputs(seed, part) draws one part's arguments, and reference() takes and returns one part's arrays. A program takes and returns all parts, laid end to end along the dimension named above; an argument that names none is the same for every part. Nothing has to cross between parts.
All inputs are finite; a program needn't handle non-finite values.
Results may differ from the reference program's by a relative error of at most 0.017.
The reference program's roundings to bfloat16 on the way count: a program that leaves them out, or rounds other values in their place, can miss the bound.
Values may be sent and summed in bfloat16 or wider, within the bound.
A program may use at most 128 MiB of HBM per device.

```python
import jax
import jax.numpy as jnp
from jax import lax

D = 128
FF = 512
HT = 16
WD = 128
WIN = 32
ROWS = 256
N_TILES = 16


def draw_features(key, part):
    base_key = jax.random.fold_in(jax.random.fold_in(key, 71), 0)
    values = jax.random.normal(base_key, (ROWS, WD, D), jnp.float32)
    return jnp.clip(values, -40.0, 40.0).astype(jnp.bfloat16)


def block_scale(key, dims, cuts, smallest, largest):
    def one(dim, shards_of):
        draws = jax.random.uniform(jax.random.fold_in(jax.random.fold_in(key, 6), dim), (shards_of,), jnp.float32, smallest / len(cuts), largest / len(cuts))
        return jnp.repeat(jnp.exp(draws), dims[dim] // shards_of).reshape((-1,) + (1,) * (len(dims) - dim - 1))

    factor_of = one(*cuts[0])
    for cut in cuts[1:]:
        factor_of = factor_of * one(*cut)
    return factor_of


def bell_draw(stream_key, extent, scale, reach, cuts=(), kind=jnp.bfloat16):
    drawn = jax.random.normal(stream_key, extent, jnp.float32) * scale
    if len(cuts) > 0:
        drawn = block_scale(stream_key, extent, cuts, -0.22, 0.18) * drawn
    return jnp.clip(drawn, min=-reach, max=reach).astype(kind)


def setup_inputs(seed: int = 0, part: int = 0) -> dict:
    streams_of = jax.random.split(jax.random.key(seed), 11)
    own_keys = jax.random.split(jax.random.fold_in(streams_of[10], part), 11)
    features = draw_features(jax.random.fold_in(jax.random.fold_in(streams_of[10], part), 71), part)
    window_offsets = jax.random.randint(own_keys[1], (2,), 0, WIN).astype(jnp.int32)
    self_project = bell_draw(streams_of[2], (D, 3 * D), D ** -0.5, 0.5)
    self_merge = bell_draw(streams_of[3], (D, D), D ** -0.5, 0.5)
    cross_project = bell_draw(streams_of[4], (D, 3 * D), D ** -0.5, 0.5)
    cross_merge = bell_draw(streams_of[5], (D, D), D ** -0.5, 0.5)
    feed_in = bell_draw(streams_of[6], (2 * D, FF), (2 * D) ** -0.5, 0.375)
    feed_out = bell_draw(streams_of[7], (FF, D), FF ** -0.5, 0.25)
    norm_gains = jnp.clip(1.0 + 0.18 * jax.random.normal(streams_of[8], (3, D), jnp.float32), 0.1, 1.9)
    result_grad = bell_draw(own_keys[9], (ROWS, WD, D), 1.0, 6.0, ((0, 16),), jnp.float32)
    return {"features": features, "window_offsets": window_offsets, "self_project": self_project, "self_merge": self_merge, "cross_project": cross_project, "cross_merge": cross_merge, "feed_in": feed_in, "feed_out": feed_out, "norm_gains": norm_gains, "result_grad": result_grad}


NORM_EPS = 1e-05
MASK_FILL = -1000000000.0
HALF_ROOT = 0.7071067811865476
DENSITY_COEF = 0.3989422804014327

def project(inputs, weight):
    return jnp.dot(inputs, weight, preferred_element_type=jnp.float32)

def back_project(grad_rows, weight):
    return jnp.dot(grad_rows, weight.T, preferred_element_type=jnp.float32)

def weight_grad(inputs, grad_rows):
    return jnp.dot(inputs.T, grad_rows, preferred_element_type=jnp.float32)

def layer_norm(values, norm_gain):
    center = values - lax.optimization_barrier(jnp.mean(values, axis=-1, keepdims=True))
    inverse = lax.rsqrt(lax.optimization_barrier(jnp.mean(center * center, axis=-1, keepdims=True)) + NORM_EPS)
    unit_rows = center * inverse
    return (unit_rows * norm_gain, unit_rows, inverse)

def norm_backward(upstream, norm_gain, unit_rows, inverse):
    scaled = upstream * norm_gain
    value_gradient = inverse * (scaled - lax.optimization_barrier(jnp.mean(scaled, axis=-1, keepdims=True)) - unit_rows * lax.optimization_barrier(jnp.mean(scaled * unit_rows, axis=-1, keepdims=True)))
    return (value_gradient, lax.optimization_barrier(jnp.sum(upstream * unit_rows, axis=0)))

def gelu_exact(values):
    return 0.5 * values * (1.0 + lax.erf(values * HALF_ROOT))

def gelu_slope(values):
    return 0.5 * (1.0 + lax.erf(values * HALF_ROOT)) + values * jnp.exp(-0.5 * values * values) * DENSITY_COEF

def to_windows(array, row_groups, group_rows, col_groups):
    width = array.shape[-1]
    shaped = array.reshape(row_groups, group_rows, col_groups, WIN, width)
    return shaped.transpose(0, 2, 1, 3, 4).reshape(row_groups * col_groups, group_rows * WIN, width)

def from_windows(array, row_groups, group_rows, col_groups):
    width = array.shape[-1]
    shaped = array.reshape(row_groups, col_groups, group_rows, WIN, width)
    return shaped.transpose(0, 2, 1, 3, 4).reshape(row_groups * group_rows, col_groups * WIN, width)

def attention_shares(query_rows, key_matrix, key_valid, logit_scale):
    attention_logits = jnp.einsum('hcn,hzn->hcz', query_rows.astype(jnp.float32), key_matrix.astype(jnp.float32)) * logit_scale
    attention_logits = jnp.where(key_valid, attention_logits, MASK_FILL)
    top_score = lax.optimization_barrier(jnp.max(attention_logits, axis=-1, keepdims=True))
    raised = jnp.exp(attention_logits - top_score)
    shares = raised / lax.optimization_barrier(jnp.sum(raised, axis=-1, keepdims=True))
    return (shares, shares.astype(jnp.bfloat16))

def apply_shares(portion_weights, value_matrix):
    return jnp.einsum('tni,tip->tnp', portion_weights.astype(jnp.float32), value_matrix.astype(jnp.float32)).astype(jnp.bfloat16)

def shares_backward(query_rows, key_matrix, value_matrix, shares, portion_weights, mixture_gradient, logit_scale):
    float_gradient = mixture_gradient.astype(jnp.float32)
    portion_gradient = jnp.einsum('hcn,hzn->hcz', float_gradient, value_matrix.astype(jnp.float32))
    value_gradient = jnp.einsum('nvw,nvc->nwc', portion_weights.astype(jnp.float32), float_gradient)
    inner_sum = lax.optimization_barrier(jnp.sum(portion_gradient * shares, axis=-1, keepdims=True))
    logit_gradient = (shares * (portion_gradient - inner_sum) * logit_scale).astype(jnp.bfloat16).astype(jnp.float32)
    query_gradient = jnp.einsum('tni,tip->tnp', logit_gradient, key_matrix.astype(jnp.float32))
    key_gradient = jnp.einsum('nvw,nvc->nwc', logit_gradient, query_rows.astype(jnp.float32))
    return (query_gradient, key_gradient, value_gradient)

def window_layout(image_rows):
    half_rows = HT // 2
    row_groups = image_rows // HT + 1
    col_groups = WD // WIN
    row_index = jnp.arange(row_groups * HT)
    row_flags = (row_index >= half_rows) & (row_index < half_rows + image_rows)
    key_valid = jnp.broadcast_to(row_flags.reshape(row_groups, 1, HT, 1), (row_groups, col_groups, HT, WIN)).reshape(row_groups * col_groups, 1, HT * WIN)
    return (half_rows, row_groups, col_groups, key_valid)

def self_forward(one_image, offset, self_project):
    image_rows = one_image.shape[0]
    half_rows, row_groups, col_groups, key_valid = window_layout(image_rows)
    rolled = jnp.roll(one_image, -offset, axis=1)
    projected = project(rolled.reshape(-1, D), self_project).astype(jnp.bfloat16).reshape(image_rows, WD, 3 * D)
    padded = jnp.pad(projected, ((half_rows, half_rows), (0, 0), (0, 0)))
    windows = to_windows(padded, row_groups, HT, col_groups)
    shares, portion_weights = attention_shares(windows[:, :, :D], windows[:, :, D:2 * D], key_valid, D ** (-0.5))
    mixed = apply_shares(portion_weights, windows[:, :, 2 * D:])
    mixed_rows = from_windows(mixed, row_groups, HT, col_groups)[half_rows:half_rows + image_rows]
    return (jnp.roll(mixed_rows, offset, axis=1), rolled, windows, shares, portion_weights)

def self_backward(mixture_gradient, offset, windows, shares, portion_weights):
    image_rows = mixture_gradient.shape[0]
    half_rows, row_groups, col_groups, key_valid = window_layout(image_rows)
    rolled_grad = jnp.roll(mixture_gradient, -offset, axis=1)
    padded = jnp.pad(rolled_grad, ((half_rows, half_rows), (0, 0), (0, 0)))
    grad_windows = to_windows(padded, row_groups, HT, col_groups)
    query_gradient, key_gradient, value_gradient = shares_backward(windows[:, :, :D], windows[:, :, D:2 * D], windows[:, :, 2 * D:], shares, portion_weights, grad_windows, D ** (-0.5))
    combined = jnp.concatenate([query_gradient, key_gradient, value_gradient], axis=-1)
    grad_rows = from_windows(combined, row_groups, HT, col_groups)[half_rows:half_rows + image_rows]
    return grad_rows.astype(jnp.bfloat16)

def reference(features, window_offsets, self_project, self_merge, cross_project, cross_merge, feed_in, feed_out, norm_gains, result_grad):
    half_tiles = N_TILES // 2
    quarter_rows = N_TILES // 4 * HT
    image_rows = half_tiles * HT
    tile_tokens = HT * WD
    all_tokens = 2 * image_rows * WD
    logit_scale = D ** (-0.5)
    grad_scale = all_tokens ** (-0.5)
    features = jnp.roll(features, -quarter_rows, axis=0)
    result_grad = jnp.roll(result_grad, -quarter_rows, axis=0)
    flat_features = features.reshape(all_tokens, D)
    mix_list = []
    rolled_list = []
    saved_list = []
    for image_index in range(2):
        one_image = features[image_index * image_rows:(image_index + 1) * image_rows]
        mixed, rolled, windows, shares, portion_weights = self_forward(one_image, window_offsets[image_index], self_project)
        mix_list.append(mixed)
        rolled_list.append(rolled.reshape(-1, D))
        saved_list.append((windows, shares, portion_weights))
    self_mix = jnp.concatenate(mix_list, axis=0).reshape(all_tokens, D)
    rolled_flat = jnp.concatenate(rolled_list, axis=0)
    self_normed, self_unit, self_inverse = layer_norm(project(self_mix, self_merge), norm_gains[0])
    middle = (flat_features.astype(jnp.float32) + self_normed).astype(jnp.bfloat16)
    cross_query = project(middle, cross_project[:, :D]).astype(jnp.bfloat16)
    cross_keyval = project(middle, cross_project[:, D:]).astype(jnp.bfloat16)
    query_tiles = cross_query.reshape(2 * half_tiles, tile_tokens, D)
    keyval_tiles = cross_keyval.reshape(2, half_tiles, tile_tokens, 2 * D)[::-1].reshape(2 * half_tiles, tile_tokens, 2 * D)
    all_valid = jnp.ones((1, 1, tile_tokens), dtype=jnp.bool_)

    def cross_tile(pieces):
        query_tile, keyval_tile = pieces
        shares, portion_weights = attention_shares(query_tile[None], keyval_tile[None, :, :D], all_valid, logit_scale)
        return apply_shares(portion_weights, keyval_tile[None, :, D:])[0]
    cross_mix = lax.map(cross_tile, (query_tiles, keyval_tiles)).reshape(all_tokens, D)
    cross_full, cross_unit, cross_inverse = layer_norm(project(cross_mix, cross_merge), norm_gains[1])
    cross_normed = cross_full.astype(jnp.bfloat16)
    joined = jnp.concatenate([middle, cross_normed], axis=1)
    feed_pre = project(joined, feed_in)
    feed_hidden = gelu_exact(feed_pre).astype(jnp.bfloat16)
    feed_normed, feed_unit, feed_inverse = layer_norm(project(feed_hidden, feed_out), norm_gains[2])
    result = (middle.astype(jnp.float32) + feed_normed).astype(jnp.bfloat16)
    upstream = result_grad.reshape(all_tokens, D)
    grad_post_full, gain_feed = norm_backward(upstream, norm_gains[2], feed_unit, feed_inverse)
    grad_post = grad_post_full.astype(jnp.bfloat16)
    grad_pre = (back_project(grad_post, feed_out) * gelu_slope(feed_pre)).astype(jnp.bfloat16)
    grad_joined = back_project(grad_pre, feed_in)
    feed_in_grad = weight_grad(joined, grad_pre) * grad_scale
    feed_out_grad = weight_grad(feed_hidden, grad_post) * grad_scale
    grad_cross_full, gain_cross = norm_backward(grad_joined[:, D:], norm_gains[1], cross_unit, cross_inverse)
    grad_cross_merged = grad_cross_full.astype(jnp.bfloat16)
    cross_merge_grad = weight_grad(cross_mix, grad_cross_merged) * grad_scale
    grad_cross_mix = back_project(grad_cross_merged, cross_merge).astype(jnp.bfloat16)

    def cross_tile_back(pieces):
        query_tile, keyval_tile, grad_tile = pieces
        shares, portion_weights = attention_shares(query_tile[None], keyval_tile[None, :, :D], all_valid, logit_scale)
        query_gradient, key_gradient, value_gradient = shares_backward(query_tile[None], keyval_tile[None, :, :D], keyval_tile[None, :, D:], shares, portion_weights, grad_tile[None], logit_scale)
        return (query_gradient[0].astype(jnp.bfloat16), jnp.concatenate([key_gradient[0], value_gradient[0]], axis=-1).astype(jnp.bfloat16))
    grad_query_tiles, grad_keyval_tiles = lax.map(cross_tile_back, (query_tiles, keyval_tiles, grad_cross_mix.reshape(2 * half_tiles, tile_tokens, D)))
    grad_cross_query = grad_query_tiles.reshape(all_tokens, D)
    returned_keyval = grad_keyval_tiles.reshape(2, half_tiles, tile_tokens, 2 * D)[::-1].reshape(all_tokens, 2 * D)
    grad_middle = upstream + grad_joined[:, :D] + back_project(grad_cross_query, cross_project[:, :D]) + back_project(returned_keyval, cross_project[:, D:])
    cross_project_grad = jnp.concatenate([weight_grad(middle, grad_cross_query), weight_grad(middle, returned_keyval)], axis=1) * grad_scale
    grad_self_full, gain_self = norm_backward(grad_middle, norm_gains[0], self_unit, self_inverse)
    grad_self_merged = grad_self_full.astype(jnp.bfloat16)
    self_merge_grad = weight_grad(self_mix, grad_self_merged) * grad_scale
    grad_self_mix = back_project(grad_self_merged, self_merge).astype(jnp.bfloat16).reshape(2, image_rows, WD, D)
    proj_grads = []
    feature_terms = []
    for image_index in range(2):
        windows, shares, portion_weights = saved_list[image_index]
        grad_rows = self_backward(grad_self_mix[image_index], window_offsets[image_index], windows, shares, portion_weights)
        flat_grad = grad_rows.reshape(-1, 3 * D)
        proj_grads.append(flat_grad)
        term = back_project(flat_grad, self_project).reshape(image_rows, WD, D)
        feature_terms.append(jnp.roll(term, window_offsets[image_index], axis=1))
    grad_self_proj = jnp.concatenate(proj_grads, axis=0)
    self_project_grad = weight_grad(rolled_flat, grad_self_proj) * grad_scale
    features_grad = grad_middle.reshape(2 * image_rows, WD, D) + jnp.concatenate(feature_terms, axis=0)
    norm_gains_grad = jnp.stack([gain_self, gain_cross, gain_feed], axis=0) * grad_scale
    result_rows = jnp.roll(result.reshape(2 * image_rows, WD, D), quarter_rows, axis=0)
    features_grad = jnp.roll(features_grad, quarter_rows, axis=0)
    return (result_rows, features_grad, self_project_grad, self_merge_grad, cross_project_grad, cross_merge_grad, feed_in_grad, feed_out_grad, norm_gains_grad)
```

```python
import functools
import math

import jax
import jax.numpy as jnp
from jax import lax
from jax.experimental import pallas as pl
from jax.experimental.pallas import tpu as pltpu
from jax.sharding import PartitionSpec as P

WIN = 32
NORM_EPS = 1e-05
MASK_FILL = -1000000000.0
HALF_ROOT = 0.7071067811865476
DENSITY_COEF = 0.3989422804014327
VMEM_BYTES = 56 * 1024 * 1024
F32 = jnp.float32
BF16 = jnp.bfloat16


def passed_along(array, axis, by):
    length = lax.axis_size(axis)
    return lax.ppermute(array, axis, [(i, (i + by) % length) for i in range(length)])


def dot_nn(a, b):
    return lax.dot_general(a, b, (((1,), (0,)), ((), ())), preferred_element_type=F32)


def dot_nt(a, b):
    return lax.dot_general(a, b, (((1,), (1,)), ((), ())), preferred_element_type=F32)


def dot_tn(a, b):
    return lax.dot_general(a, b, (((0,), (0,)), ((), ())), preferred_element_type=F32)


def unit_norm(values):
    center = values - jnp.mean(values, axis=-1, keepdims=True)
    inverse = lax.rsqrt(jnp.mean(center * center, axis=-1, keepdims=True) + NORM_EPS)
    return center * inverse, inverse


def norm_backward(upstream, gain, unit_rows, inverse):
    scaled = upstream * gain
    return inverse * (
        scaled
        - jnp.mean(scaled, axis=-1, keepdims=True)
        - unit_rows * jnp.mean(scaled * unit_rows, axis=-1, keepdims=True)
    )


def softmax_rows(logits):
    raised = jnp.exp(logits - jnp.max(logits, axis=-1, keepdims=True))
    return raised * (1.0 / jnp.sum(raised, axis=-1, keepdims=True))


def window_keep(valid_ref, cols, own, tokens):
    group = pl.program_id(0) // cols
    flag = valid_ref[group]
    column = lax.broadcasted_iota(jnp.int32, (1, tokens), 1)
    return (column < own) | (flag > 0)


def self_forward_kernel(
    cols, valid_ref, own_ref, halo_ref, weight_ref, merge_ref, gains_ref, mix_ref, middle_ref
):
    d = own_ref.shape[1]
    count = own_ref.shape[0]
    own = own_ref[...]
    own_proj = dot_nn(own, weight_ref[...]).astype(BF16)
    halo_kv = dot_nn(halo_ref[...], weight_ref[:, d:]).astype(BF16)
    keys = jnp.concatenate([own_proj[:, d : 2 * d], halo_kv[:, :d]], axis=0)
    values = jnp.concatenate([own_proj[:, 2 * d :], halo_kv[:, d:]], axis=0)
    logits = dot_nt(own_proj[:, :d], keys) * d**-0.5
    logits = jnp.where(window_keep(valid_ref, cols, count, 2 * count), logits, MASK_FILL)
    weights = softmax_rows(logits).astype(BF16)
    mix = dot_nn(weights, values).astype(BF16)
    unit, _ = unit_norm(dot_nn(mix, merge_ref[...]))
    mix_ref[...] = mix
    middle_ref[...] = (own.astype(F32) + unit * gains_ref[0:1, :]).astype(BF16)


def cross_kernel(
    scale,
    middle_ref,
    partner_ref,
    upstream_ref,
    project_ref,
    merge_ref,
    feed_in_ref,
    feed_out_ref,
    gains_ref,
    result_ref,
    partial_ref,
    term_ref,
    g_project_ref,
    g_merge_ref,
    g_in_ref,
    g_out_ref,
    g_gain_ref,
    key_ref,
    value_ref,
    dkey_ref,
    dvalue_ref,
):
    step = pl.program_id(0)
    d = middle_ref.shape[1]

    @pl.when(step == 0)
    def _():
        keyval = dot_nn(partner_ref[...], project_ref[:, d:]).astype(BF16)
        key_ref[...] = keyval[:, :d]
        value_ref[...] = keyval[:, d:]
        for ref in (
            dkey_ref,
            dvalue_ref,
            g_project_ref,
            g_merge_ref,
            g_in_ref,
            g_out_ref,
            g_gain_ref,
        ):
            ref[...] = jnp.zeros(ref.shape, ref.dtype)

    middle = middle_ref[...]
    query = dot_nn(middle, project_ref[:, :d]).astype(BF16)
    keys = key_ref[...]
    values = value_ref[...]
    shares = softmax_rows(dot_nt(query, keys) * d**-0.5)
    weights = shares.astype(BF16)
    mix = dot_nn(weights, values).astype(BF16)
    unit_cross, inverse_cross = unit_norm(dot_nn(mix, merge_ref[...]))
    normed = (unit_cross * gains_ref[1:2, :]).astype(BF16)
    joined = jnp.concatenate([middle, normed], axis=1)
    pre = dot_nn(joined, feed_in_ref[...])
    bell = 0.5 * (1.0 + lax.erf(pre * HALF_ROOT))
    hidden = (pre * bell).astype(BF16)
    slope = bell + pre * jnp.exp(-0.5 * pre * pre) * DENSITY_COEF
    unit_feed, inverse_feed = unit_norm(dot_nn(hidden, feed_out_ref[...]))
    result_ref[...] = (middle.astype(F32) + unit_feed * gains_ref[2:3, :]).astype(BF16)
    upstream = upstream_ref[...]
    post = norm_backward(upstream, gains_ref[2:3, :], unit_feed, inverse_feed).astype(BF16)
    g_gain_ref[1:2, :] += jnp.sum(upstream * unit_feed, axis=0, keepdims=True) * scale
    grad_pre = (dot_nt(post, feed_out_ref[...]) * slope).astype(BF16)
    grad_joined = dot_nt(grad_pre, feed_in_ref[...])
    g_in_ref[...] += dot_tn(joined, grad_pre) * scale
    g_out_ref[...] += dot_tn(hidden, post) * scale
    grad_normed = grad_joined[:, d:]
    merged = norm_backward(grad_normed, gains_ref[1:2, :], unit_cross, inverse_cross).astype(BF16)
    g_gain_ref[0:1, :] += jnp.sum(grad_normed * unit_cross, axis=0, keepdims=True) * scale
    g_merge_ref[...] += dot_tn(mix, merged) * scale
    grad_mix = dot_nt(merged, merge_ref[...]).astype(BF16)
    portion = dot_nt(grad_mix, values)
    inner = jnp.sum(portion * shares, axis=-1, keepdims=True)
    scores = (shares * (portion - inner) * d**-0.5).astype(BF16)
    dvalue_ref[...] += dot_tn(weights, grad_mix)
    dkey_ref[...] += dot_tn(scores, query)
    grad_query = dot_nn(scores, keys).astype(BF16)
    g_project_ref[:, :d] += dot_tn(middle, grad_query) * scale
    partial_ref[...] = (
        upstream + grad_joined[:, :d] + dot_nt(grad_query, project_ref[:, :d])
    )

    @pl.when(step == pl.num_programs(0) - 1)
    def _():
        grad_kv = jnp.concatenate(
            [dkey_ref[...].astype(BF16), dvalue_ref[...].astype(BF16)], axis=1
        )
        term_ref[...] = dot_nt(grad_kv, project_ref[:, d:]).astype(BF16)
        g_project_ref[:, d:] = dot_tn(partner_ref[...], grad_kv) * scale


def merge_backward_kernel(
    scale,
    partial_ref,
    term_ref,
    mix_ref,
    merge_ref,
    gains_ref,
    middle_grad_ref,
    mix_grad_ref,
    g_merge_ref,
    g_gain_ref,
):
    @pl.when(pl.program_id(0) == 0)
    def _():
        g_merge_ref[...] = jnp.zeros(g_merge_ref.shape, F32)
        g_gain_ref[...] = jnp.zeros(g_gain_ref.shape, F32)

    grad = partial_ref[...] + term_ref[...].astype(F32)
    mix = mix_ref[...]
    unit, inverse = unit_norm(dot_nn(mix, merge_ref[...]))
    merged = norm_backward(grad, gains_ref[0:1, :], unit, inverse).astype(BF16)
    g_gain_ref[0:1, :] += jnp.sum(grad * unit, axis=0, keepdims=True) * scale
    g_merge_ref[...] += dot_tn(mix, merged) * scale
    middle_grad_ref[...] = grad
    mix_grad_ref[...] = dot_nt(merged, merge_ref[...]).astype(BF16)


def self_backward_kernel(
    cols,
    scale,
    valid_ref,
    own_ref,
    halo_ref,
    own_grad_ref,
    halo_grad_ref,
    middle_grad_ref,
    weight_ref,
    grad_ref,
    g_weight_ref,
):
    @pl.when(pl.program_id(0) == 0)
    def _():
        g_weight_ref[...] = jnp.zeros(g_weight_ref.shape, F32)

    d = own_ref.shape[1]
    count = own_ref.shape[0]
    flag = valid_ref[pl.program_id(0) // cols]
    own = own_ref[...]
    proj = dot_nn(jnp.concatenate([own, halo_ref[...]], axis=0), weight_ref[...]).astype(BF16)
    queries = proj[:, :d]
    keys = proj[:, d : 2 * d]
    values = proj[:, 2 * d :]
    halo_grad = jnp.where(flag > 0, halo_grad_ref[...].astype(F32), 0.0).astype(BF16)
    mix_grad = jnp.concatenate([own_grad_ref[...], halo_grad], axis=0)
    logits = dot_nt(queries, keys) * d**-0.5
    logits = jnp.where(window_keep(valid_ref, cols, count, 2 * count), logits, MASK_FILL)
    shares = softmax_rows(logits)
    portion = dot_nt(mix_grad, values)
    inner = jnp.sum(portion * shares, axis=-1, keepdims=True)
    scores = (shares * (portion - inner) * d**-0.5).astype(BF16)
    grad_query = dot_nn(scores[:count], keys)
    grad_key = dot_tn(scores[:, :count], queries)
    grad_value = dot_tn(shares[:, :count].astype(BF16), mix_grad)
    grad_proj = jnp.concatenate(
        [grad_query.astype(BF16), grad_key.astype(BF16), grad_value.astype(BF16)], axis=1
    )
    grad_ref[...] = middle_grad_ref[...] + dot_nt(grad_proj, weight_ref[...])
    g_weight_ref[...] += dot_tn(own, grad_proj) * scale


def rows_spec(rows, d):
    return pl.BlockSpec((rows, d), lambda i: (i, 0))


def whole_spec(array):
    return pl.BlockSpec(array.shape, lambda i: (0, 0))


SMEM_SPEC = pl.BlockSpec(memory_space=pltpu.SMEM)


def call(kernel, grid, in_specs, outs, scratch, flops, args):
    return pl.pallas_call(
        kernel,
        grid=(grid,),
        in_specs=in_specs,
        out_specs=[spec for spec, _ in outs],
        out_shape=[shape for _, shape in outs],
        scratch_shapes=scratch,
        compiler_params=pltpu.CompilerParams(
            dimension_semantics=("arbitrary",), vmem_limit_bytes=VMEM_BYTES
        ),
        cost_estimate=pl.CostEstimate(flops=flops, bytes_accessed=4_000_000, transcendentals=0),
    )(*args)


def tokens_out(rows, tokens, d, kind):
    return (rows_spec(rows, d), jax.ShapeDtypeStruct((tokens, d), kind))


def total_out(rows, columns):
    return (
        pl.BlockSpec((rows, columns), lambda i: (0, 0)),
        jax.ShapeDtypeStruct((rows, columns), F32),
    )


def to_windows(array, offset, cols):
    rows, width, d = array.shape
    half = rows // 2
    rolled = jnp.roll(array, -offset, axis=1).reshape(2, half, cols, WIN, d)
    return rolled.transpose(0, 2, 1, 3, 4).reshape(rows * width, d)


def from_windows(array, offset, cols, rows, width):
    d = array.shape[-1]
    half = rows // 2
    shaped = array.reshape(2, cols, half, WIN, d).transpose(0, 2, 1, 3, 4)
    return jnp.roll(shaped.reshape(rows, width, d), offset, axis=1)


def scatter_sum(arrays):
    count = lax.axis_size("tiles")
    flat = [a.reshape(count, -1) for a in arrays]
    joined = jnp.concatenate(flat, axis=1).astype(BF16)
    parts = lax.all_to_all(joined, "tiles", split_axis=0, concat_axis=0, tiled=True)
    total = jnp.sum(parts.astype(F32), axis=0)
    pieces = []
    start = 0
    for a in arrays:
        size = a.size // count
        pieces.append(total[start : start + size].reshape(a.shape[0] // count, -1))
        start += size
    return pieces


def body(
    features,
    window_offsets,
    self_project,
    self_merge,
    cross_project,
    cross_merge,
    feed_in,
    feed_out,
    norm_gains,
    result_grad,
):
    rows, width, d = features.shape
    hidden = feed_in.shape[1]
    tokens = rows * width
    half_tokens = tokens // 2
    cols = width // WIN
    windows = 2 * cols
    per_window = tokens // windows
    count = lax.axis_size("tiles")
    half_tiles = count // 2
    position = lax.axis_index("tiles")
    place = (position + count - count // 4) % count
    offset = window_offsets[place // half_tiles]
    scale = 1.0 / math.sqrt(count * tokens)
    valid = jnp.stack(
        [place % half_tiles != 0, place % half_tiles != half_tiles - 1]
    ).astype(jnp.int32)

    own = to_windows(features, offset, cols)

    def halo_of(array):
        above = passed_along(array[half_tokens:], "tiles", 1)
        below = passed_along(array[:half_tokens], "tiles", -1)
        return jnp.concatenate([above, below], axis=0)

    halo = halo_of(own)
    upstream = to_windows(result_grad, offset, cols)
    window_spec = rows_spec(per_window, d)
    self_mix, middle = call(
        functools.partial(self_forward_kernel, cols),
        windows,
        [
            SMEM_SPEC,
            window_spec,
            window_spec,
            whole_spec(self_project),
            whole_spec(self_merge),
            whole_spec(norm_gains),
        ],
        [tokens_out(per_window, tokens, d, BF16), tokens_out(per_window, tokens, d, BF16)],
        [],
        2_000_000_000,
        (valid, own, halo, self_project, self_merge, norm_gains),
    )
    partner = passed_along(middle, "tiles", half_tiles)
    block = min(256, tokens)
    block_spec = rows_spec(block, d)
    result, partial, term, g_cross, g_cross_merge, g_in, g_out, g_gain = call(
        functools.partial(cross_kernel, scale),
        tokens // block,
        [
            block_spec,
            whole_spec(partner),
            block_spec,
            whole_spec(cross_project),
            whole_spec(cross_merge),
            whole_spec(feed_in),
            whole_spec(feed_out),
            whole_spec(norm_gains),
        ],
        [
            tokens_out(block, tokens, d, BF16),
            tokens_out(block, tokens, d, F32),
            (
                pl.BlockSpec((tokens, d), lambda i: (0, 0)),
                jax.ShapeDtypeStruct((tokens, d), BF16),
            ),
            total_out(d, 3 * d),
            total_out(d, d),
            total_out(2 * d, hidden),
            total_out(hidden, d),
            total_out(2, d),
        ],
        [
            pltpu.VMEM((tokens, d), BF16),
            pltpu.VMEM((tokens, d), BF16),
            pltpu.VMEM((tokens, d), F32),
            pltpu.VMEM((tokens, d), F32),
        ],
        14_000_000_000,
        (middle, partner, upstream, cross_project, cross_merge, feed_in, feed_out, norm_gains),
    )
    returned = passed_along(term, "tiles", half_tiles)
    s_in, s_out, s_cross, s_cross_merge = scatter_sum([g_in, g_out, g_cross, g_cross_merge])
    result = from_windows(result, offset, cols, rows, width)
    middle_grad, mix_grad, g_merge, g_gain_self = call(
        functools.partial(merge_backward_kernel, scale),
        tokens // block,
        [
            block_spec,
            block_spec,
            block_spec,
            whole_spec(self_merge),
            whole_spec(norm_gains),
        ],
        [
            tokens_out(block, tokens, d, F32),
            tokens_out(block, tokens, d, BF16),
            total_out(d, d),
            total_out(1, d),
        ],
        [],
        400_000_000,
        (partial, returned, self_mix, self_merge, norm_gains),
    )
    halo_grad = halo_of(mix_grad)
    grad_windows, g_self = call(
        functools.partial(self_backward_kernel, cols, scale),
        windows,
        [
            SMEM_SPEC,
            window_spec,
            window_spec,
            window_spec,
            window_spec,
            window_spec,
            whole_spec(self_project),
        ],
        [tokens_out(per_window, tokens, d, F32), total_out(d, 3 * d)],
        [],
        5_000_000_000,
        (valid, own, halo, mix_grad, halo_grad, middle_grad, self_project),
    )
    gains = jnp.concatenate([g_gain_self, g_gain], axis=0)
    gains = gains.reshape(3, count, d // count).transpose(1, 0, 2).reshape(count, -1)
    s_self, s_merge, s_gains = scatter_sum([g_self, g_merge, gains])
    features_grad = from_windows(grad_windows, offset, cols, rows, width)
    return (
        result,
        features_grad,
        s_self.reshape(d // count, 3 * d),
        s_merge.reshape(d // count, d),
        s_cross.reshape(d // count, 3 * d),
        s_cross_merge.reshape(d // count, d),
        s_in.reshape(2 * d // count, hidden),
        s_out.reshape(hidden // count, d),
        s_gains.reshape(3, d // count),
    )


def solution(mesh):
    rows3 = P(("groups", "tiles"), None, None)
    rows2 = P(("groups", "tiles"), None)
    return jax.shard_map(
        body,
        mesh=mesh,
        in_specs=(rows3, P("groups")) + (P(),) * 7 + (rows3,),
        out_specs=(rows3, rows3) + (rows2,) * 6 + (P("groups", "tiles"),),
        check_vma=False,
    )
```
